32 devices in a mesh: groups: 2 (over y), rows: 4 (over z), cols: 4 (over x, core).
Axes of the slice: x: 2, y: 2, z: 4, core: 2. Of those that a mesh axis runs over, the one named last changes fastest.
Arguments:
- pair: float32 [512, 256, 128], P(('groups', 'rows'), 'cols'), parts along dimension 0, may hold values from -6 to 6
- pair_mask: int32 [512, 256], P(('groups', 'rows'), 'cols'), parts along dimension 0, may hold values 0 or 1
- in_gain: float32 [128], replicated, may hold values from 0.1 to 1.9
- in_bias: float32 [128], replicated, may hold values from -3 to 3
- proj_weight: bfloat16 [128, 512], replicated, may hold values from -0.5 to 0.5
- gate_weight: bfloat16 [128, 128], replicated, may hold values from -0.5 to 0.5
- out_gain: float32 [128], replicated, may hold values from 0.1 to 1.9
- out_bias: float32 [128], replicated, may hold values from -3 to 3
- out_weight: bfloat16 [128, 128], replicated, may hold values from -0.5 to 0.5
Outputs:
- update: float32 [512, 256, 128], P(('groups', 'rows'), 'cols'), parts along dimension 0
The draws below stay inside these ranges and needn't reach their ends.
There are 2 independent parts, one for each index of `groups`. The reference program is written for one: setup_inputs(seed, part) draws one part's arguments, and reference() takes and returns one part's arrays. A program takes and returns all parts, laid end to end along the dimension named above; an argument that names none is the same for every part. Nothing has to cross between parts.
Inputs may be any that keep to these rules, and one draw needn't show every extreme that they name: `pair_mask`: 1 where a pair of residues takes part, else 0.
All inputs are finite; a program needn't handle non-finite values. No bound on the sum of `pair_mask` on one device may be relied on, other than what follows from the above.
Results may differ from the reference program's by a relative error of at most 0.0052.
Values may be sent and summed in bfloat16 or wider, within the bound.
No kernel may reach another device: no remote copies, remote signals or barrier semaphores. Data moves between devices by JAX's collectives and lax.ppermute only.
A program may use at most 64 MiB of HBM per device.

```python
import jax
import jax.numpy as jnp
from jax import lax

C = 128
N = 256


def place_ends(array, own_key, low, top_value):
    spot = [jax.random.randint(jax.random.fold_in(own_key, axis), (), 0, length) for axis, length in enumerate(array.shape)]
    widest = array.shape.index(max(array.shape))
    neighbour = spot[:widest] + [(spot[widest] + 1) % array.shape[widest]] + spot[widest + 1:]
    return array.at[tuple(spot)].set(low).at[tuple(neighbour)].set(top_value)


def steps_of(key, shape, shards, low, high):
    level, own = 1.0, jax.random.fold_in(key, 6)
    for axis_at, blocks in shards:
        draws = jnp.exp(jax.random.uniform(jax.random.fold_in(own, axis_at), (blocks,), jnp.float32, low / len(shards), high / len(shards)))
        level = level * jnp.repeat(draws, shape[axis_at] // blocks).reshape([-1 if axis == axis_at else 1 for axis in range(len(shape))])
    return level


def normal_values(key, dims, deviation, bound, split=(), kind=jnp.bfloat16):
    array = deviation * jax.random.normal(key, dims, jnp.float32)
    if split:
        array = array * steps_of(key, dims, split, -0.22, 0.18)
    return jnp.clip(array, -bound, bound).astype(kind)


def setup_inputs(seed: int = 0, part: int = 0) -> dict:
    streams_of = jax.random.split(jax.random.key(seed), 10)
    part_splits = jax.random.split(jax.random.fold_in(streams_of[9], part), 10)
    return {
        "pair": normal_values(part_splits[0], (N, N, C), 1.0, 6.0, ((0, 4), (1, 4)), jnp.float32),
        "pair_mask": place_ends((jax.random.randint(part_splits[1], (N, N), 0, 8) < 7).astype(jnp.int32), jax.random.fold_in(part_splits[1], 1), 0, 1),
        "in_gain": jnp.clip(1.0 + 0.18 * jax.random.normal(streams_of[2], (C,), jnp.float32), 0.1, 1.9),
        "in_bias": normal_values(streams_of[3], (C,), 0.5, 3.0, (), jnp.float32),
        "proj_weight": normal_values(streams_of[4], (C, 4 * C), C ** -0.5, 0.5),
        "gate_weight": normal_values(streams_of[5], (C, C), C ** -0.5, 0.5),
        "out_gain": jnp.clip(1.0 + 0.18 * jax.random.normal(streams_of[6], (C,), jnp.float32), 0.1, 1.9),
        "out_bias": normal_values(streams_of[7], (C,), 0.5, 3.0, (), jnp.float32),
        "out_weight": normal_values(streams_of[8], (C, C), C ** -0.5, 0.5),
    }


def layer_norm(values, gain, shift, axis):
    mean = lax.optimization_barrier(jnp.mean(values, axis=axis, keepdims=True))
    centered = values - mean
    spread = lax.optimization_barrier(jnp.mean(centered * centered, axis=axis, keepdims=True))
    return centered * lax.rsqrt(spread + 1e-05) * gain + shift

def gated_side(normed_rows, weights, keep):
    channels = weights.shape[0]
    values = jnp.dot(normed_rows, weights, preferred_element_type=jnp.float32)
    return (jax.nn.sigmoid(values[:, channels:]) * values[:, :channels] * keep).astype(jnp.bfloat16)

def multiply(operands):
    left, right = operands
    result = jnp.einsum('cik,cjk->cij', left.astype(jnp.float32), right.astype(jnp.float32), precision=lax.Precision.HIGHEST)
    return result.astype(jnp.bfloat16)

def reference(pair, pair_mask, in_gain, in_bias, proj_weight, gate_weight, out_gain, out_bias, out_weight):
    count = pair.shape[0]
    channels = pair.shape[2]
    normed = layer_norm(pair, in_gain, in_bias, -1).astype(jnp.bfloat16).reshape(count * count, channels)
    keep = pair_mask.astype(jnp.float32).reshape(count * count, 1)
    side_a = gated_side(normed, proj_weight[:, :2 * channels], keep).reshape(count, count, channels)
    side_b = gated_side(normed, proj_weight[:, 2 * channels:], keep).reshape(count, count, channels)
    gating = jax.nn.sigmoid(jnp.dot(normed, gate_weight, preferred_element_type=jnp.float32))
    first = jnp.transpose(side_a, (2, 0, 1)).reshape(channels // 8, 8, count, count)
    second = jnp.transpose(side_b, (2, 0, 1)).reshape(channels // 8, 8, count, count)
    product = lax.map(multiply, (first, second)).reshape(channels, count, count)
    product = jnp.transpose(product, (1, 2, 0)).reshape(count * count, channels).astype(jnp.float32)
    normed_out = layer_norm(product, out_gain, out_bias, -1).astype(jnp.bfloat16)
    update = jnp.dot(normed_out, out_weight, preferred_element_type=jnp.float32) * gating
    return update.reshape(count, count, channels)
```

```python
import functools

import jax
import jax.numpy as jnp
from jax import lax
from jax.experimental import pallas as pl
from jax.experimental.pallas import tpu as pltpu
from jax.sharding import PartitionSpec as P

EPS = 1e-05
VMEM = pl.BlockSpec(memory_space=pltpu.VMEM)
LIMIT = 48 * 1024 * 1024


def call(body, out_shape, grid, in_specs, out_specs, scratch, flops, moved):
    return pl.pallas_call(
        body,
        out_shape=out_shape,
        grid=grid,
        in_specs=in_specs,
        out_specs=out_specs,
        scratch_shapes=scratch,
        compiler_params=pltpu.CompilerParams(vmem_limit_bytes=LIMIT),
        cost_estimate=pl.CostEstimate(flops=flops, bytes_accessed=moved, transcendentals=0),
    )


def sigmoid(values):
    return 0.5 * jnp.tanh(0.5 * values) + 0.5


def dot(left, right, dims):
    return lax.dot_general(left, right, (dims, ((), ())), preferred_element_type=jnp.float32)


def normalise(values, gain, shift):
    mean = jnp.mean(values, axis=-1, keepdims=True)
    centered = values - mean
    spread = jnp.mean(centered * centered, axis=-1, keepdims=True)
    return centered * lax.rsqrt(spread + EPS) * gain + shift


def norm_body(pair_ref, mask_ref, gain_ref, shift_ref, out_ref):
    keep = mask_ref[...].astype(jnp.float32).T
    gain, shift = gain_ref[...], shift_ref[...]
    for row in range(pair_ref.shape[0]):
        normed = normalise(pair_ref[row], gain, shift)
        out_ref[row] = (normed * keep[:, row : row + 1]).astype(jnp.bfloat16)


def masked_norm(pair, mask, gain, shift, step=16):
    rows, cols, channels = pair.shape
    return call(
        norm_body,
        jax.ShapeDtypeStruct(pair.shape, jnp.bfloat16),
        (rows // step,),
        [
            pl.BlockSpec((step, cols, channels), lambda g: (g, 0, 0)),
            pl.BlockSpec((step, cols), lambda g: (g, 0)),
            VMEM,
            VMEM,
        ],
        pl.BlockSpec((step, cols, channels), lambda g: (g, 0, 0)),
        [],
        10 * pair.size,
        6 * pair.size,
    )(pair, mask, gain, shift)


def gate_body(pair_ref, gain_ref, shift_ref, weight_ref, out_ref):
    rows, cols, channels = pair_ref.shape
    normed = normalise(pair_ref[...].reshape(rows * cols, channels), gain_ref[...], shift_ref[...])
    values = dot(normed.astype(jnp.bfloat16), weight_ref[...], ((1,), (0,)))
    out_ref[...] = sigmoid(values).reshape(rows, cols, channels)


def output_gate(pair, gain, shift, weight, step=8):
    rows, cols, channels = pair.shape
    return call(
        gate_body,
        jax.ShapeDtypeStruct(pair.shape, jnp.float32),
        (rows // step,),
        [pl.BlockSpec((step, cols, channels), lambda g: (g, 0, 0)), VMEM, VMEM, VMEM],
        pl.BlockSpec((step, cols, channels), lambda g: (g, 0, 0)),
        [],
        2 * pair.size * channels,
        8 * pair.size,
    )(pair, gain, shift, weight)


def side_body(own_ref, other_ref, weight_ref, out_ref, held):
    step, cols, _ = own_ref.shape
    half = out_ref.shape[0]
    weight = weight_ref[...]
    for row in range(step):
        normed = jnp.concatenate([own_ref[row], other_ref[row]], axis=0)
        values = dot(weight, normed, ((1,), (1,)))
        held[pl.ds(row, half, stride=step), :] = sigmoid(values[half:]) * values[:half]
    out_ref[...] = held[...].reshape(half, step, 2 * cols).astype(jnp.bfloat16)


def side(own, other, weight, step=16):
    rows, cols, channels = own.shape
    half = weight.shape[0] // 2
    block = pl.BlockSpec((step, cols, channels), lambda g: (g, 0, 0))
    return call(
        side_body,
        jax.ShapeDtypeStruct((half, rows, 2 * cols), jnp.bfloat16),
        (rows // step,),
        [block, block, VMEM],
        pl.BlockSpec((half, step, 2 * cols), lambda g: (0, g, 0)),
        [pltpu.VMEM((half * step, 2 * cols), jnp.float32)],
        8 * rows * cols * channels * half,
        4 * own.size + 4 * rows * cols * half,
    )(own, other, weight)


def triangle_body(first_ref, second_ref, out_ref):
    rows, deep = second_ref.shape[2:]
    zero = jnp.zeros((rows, deep), jnp.bfloat16)
    for at in range(out_ref.shape[0]):
        left = jnp.concatenate([first_ref[0, at], first_ref[1, at]], axis=1)
        right = jnp.concatenate(
            [
                jnp.concatenate([second_ref[0, at], zero], axis=1),
                jnp.concatenate([zero, second_ref[1, at]], axis=1),
            ],
            axis=0,
        )
        out_ref[at] = dot(left, right, ((1,), (1,))).astype(jnp.bfloat16)


def triangle(first, second, step=16):
    half, rows, deep = first.shape
    pairs = half // 2
    step = min(step, pairs)
    block = pl.BlockSpec((2, step, rows, deep), lambda g: (0, g, 0, 0))
    return call(
        triangle_body,
        jax.ShapeDtypeStruct((pairs, rows, 2 * rows), jnp.bfloat16),
        (pairs // step,),
        [block, block],
        pl.BlockSpec((step, rows, 2 * rows), lambda g: (g, 0, 0)),
        [],
        4 * half * rows * rows * deep,
        6 * first.size,
    )(first.reshape(2, pairs, rows, deep), second.reshape(2, pairs, rows, deep))


def finish_body(counts, *refs):
    flag_ref, parts, rest = refs[0], refs[1 : 1 + 2 * sum(counts)], refs[1 + 2 * sum(counts) :]
    gain_ref, shift_ref, weight_ref, gate_ref, out_ref, held = rest
    pairs, step, lanes = parts[0].shape
    width = lanes // 2
    early = flag_ref[0] == 1
    chunks = []
    at = 0
    for count in counts:
        total = None
        for _ in range(count):
            term = jnp.where(early, parts[at][...], parts[at + 1][...]).astype(jnp.float32)
            total = term if total is None else total + term
            at += 2
        chunks.append(total)
    total = jnp.concatenate(chunks, axis=0)
    planes = 2 * pairs

    def mean(values):
        added = jnp.sum(values, axis=0)
        return (added + pltpu.roll(added, width, 1)) * (1.0 / (2 * planes))

    centered = total - mean(total)[None]
    scale = lax.rsqrt(mean(centered * centered) + EPS)[None]
    normed = centered * scale * gain_ref[...] + shift_ref[...]
    for plane in range(planes):
        held[pl.ds(plane, step, stride=planes), :] = normed[plane]
    weight = weight_ref[...]
    for row in range(step):
        tile = held[row * planes : (row + 1) * planes, :].T.astype(jnp.bfloat16)
        update = dot(tile[:width], weight[:planes], ((1,), (0,)))
        update += dot(tile[width:], weight[planes:], ((1,), (0,)))
        out_ref[row] = update * gate_ref[row]


def finish(flag, halves, gain, shift, weight, gate, step=8):
    rows, cols, channels = gate.shape
    parts = [array for half in halves for pair in half for array in pair]
    pairs, _, lanes = parts[0].shape
    block = pl.BlockSpec((pairs, step, lanes), lambda g: (0, g, 0))
    tile = pl.BlockSpec((step, cols, channels), lambda g: (g, 0, 0))
    return call(
        functools.partial(finish_body, [len(half) for half in halves]),
        jax.ShapeDtypeStruct(gate.shape, jnp.float32),
        (rows // step,),
        [pl.BlockSpec(memory_space=pltpu.SMEM)] + [block] * len(parts) + [VMEM, VMEM, VMEM, tile],
        tile,
        [pltpu.VMEM((2 * pairs * step, lanes), jnp.float32)],
        2 * gate.size * channels,
        8 * gate.size,
    )(flag, *parts, gain, shift, weight, gate)


def planes_of(vector, width):
    pairs = vector.shape[0] // 4
    ordered = vector.reshape(2, 2, pairs).transpose(0, 2, 1).reshape(2 * pairs, 2)
    return jnp.repeat(ordered, width, axis=1)[:, None, :]


def per_device(
    mesh_rows,
    mesh_cols,
    pair,
    pair_mask,
    in_gain,
    in_bias,
    proj_weight,
    gate_weight,
    out_gain,
    out_bias,
    out_weight,
):
    rows, cols, channels = pair.shape
    half = channels // 2
    row, col = lax.axis_index("rows"), lax.axis_index("cols")
    core = col % 2
    both = ("rows", "cols")
    flip = [(at, at ^ 1) for at in range(mesh_cols)]

    weights = proj_weight.reshape(channels, 4, 2, half)
    weights = jnp.where(core == 0, weights[:, :, 0], weights[:, :, 1])
    weights = weights.transpose(1, 2, 0).reshape(2, 2 * half, channels)
    swap = lambda array: jnp.where(core == 0, array, jnp.roll(array, half, axis=0))
    last_gain, last_shift = planes_of(swap(out_gain), cols), planes_of(swap(out_bias), cols)
    last_weight = swap(out_weight).reshape(2, 2, half // 2, channels).transpose(1, 0, 2, 3)
    last_weight = last_weight.reshape(channels, channels)
    gain, shift = in_gain[None], in_bias[None]

    own = masked_norm(pair, pair_mask, gain, shift)
    other = lax.ppermute(own, "cols", flip)
    side_b = side(own, other, weights[1])

    if mesh_rows == 4 and mesh_cols == 4:
        swap_ends = [(0, 1), (1, 0), (2, 3), (3, 2)]
        swap_mid = [(1, 2), (2, 1)]
        to_ends = [(1, 0), (2, 3)]
        near_mid = lax.ppermute(side_b, "rows", swap_mid)
        partner = lax.ppermute(side_b, "rows", swap_ends)
        side_a = side(own, other, weights[0])
        gate = output_gate(pair, gain, shift, gate_weight)
        far_mid = lax.ppermute(partner, "rows", swap_mid)
        near_end = lax.ppermute(near_mid, "rows", to_ends)
        far_end = lax.ppermute(far_mid, "rows", to_ends)
        middle = (row == 1) | (row == 2)
        near = jnp.where(middle, near_mid, near_end)
        far = jnp.where(middle, far_mid, far_end)

        def spread(blocks, target):
            same = jnp.where(core == 0, blocks[0], blocks[1])
            cross = jnp.where(core == 0, blocks[1], blocks[0])
            at = lambda z, x, h: z * 4 + 2 * x + h
            places = [(z, h) for z in range(4) for h in range(2)]
            straight = [(at(z, 1 - target(z), h), at(z, target(z), h)) for z, h in places]
            diagonal = [(at(z, 1 - target(z), h), at(z, target(z), 1 - h)) for z, h in places]
            beside = [(at(z, target(z), h), at(z, target(z), 1 - h)) for z, h in places]
            return (
                same,
                lax.ppermute(same, both, straight),
                lax.ppermute(cross, both, beside),
                lax.ppermute(cross, both, diagonal),
            )

        product_own, product_partner = triangle(side_a, side_b), triangle(side_a, partner)
        even = row % 2 == 0
        early = spread(
            (
                jnp.where(even, product_own, product_partner),
                jnp.where(even, product_partner, product_own),
            ),
            lambda z: z // 2,
        )
        product_near, product_far = triangle(side_a, near), triangle(side_a, far)
        low = row < 2
        late = spread(
            (
                jnp.where(low, product_near, product_far),
                jnp.where(low, product_far, product_near),
            ),
            lambda z: 1 - z // 2,
        )
        flag = (col // 2 == row // 2).astype(jnp.int32)[None]
        halves = [
            [(early[0], late[0]), (early[1], late[1])],
            [(early[2], late[2]), (early[3], late[3])],
        ]
    else:
        side_a = side(own, other, weights[0])
        gate = output_gate(pair, gain, shift, gate_weight)
        gathered = lax.all_gather(side_b, "rows")
        products = jnp.stack([triangle(side_a, gathered[at]) for at in range(mesh_rows)])
        parts = lax.all_to_all(products, "cols", 0, 0, tiled=True).astype(jnp.float32)
        parts = jnp.sum(parts.reshape(mesh_cols // 2, 2, *parts.shape[1:]), axis=0)
        mine = jnp.where(core == 0, parts[0], parts[1])
        others = jnp.where(core == 0, parts[1], parts[0])
        flag = jnp.ones((1,), jnp.int32)
        halves = [[(mine, mine)], [(others, others)]]
    return finish(flag, halves, last_gain, last_shift, last_weight, gate)


def solution(mesh):
    tile = P(("groups", "rows"), "cols", None)
    return jax.shard_map(
        functools.partial(per_device, mesh.shape["rows"], mesh.shape["cols"]),
        mesh=mesh,
        in_specs=(tile, P(("groups", "rows"), "cols")) + (P(),) * 7,
        out_specs=tile,
        check_vma=False,
    )
```

```python
import functools

import jax
import jax.numpy as jnp
from jax import lax
from jax.experimental import pallas as pl
from jax.experimental.pallas import tpu as pltpu
from jax.sharding import PartitionSpec as P

EPS = 1e-05
VMEM = pl.BlockSpec(memory_space=pltpu.VMEM)
SMEM = pl.BlockSpec(memory_space=pltpu.SMEM)
HBM = pl.BlockSpec(memory_space=pltpu.HBM)
LIMIT = 24 * 1024 * 1024
STEP = 16
CHUNKS = 4


def call(body, out_shape, in_specs, out_specs, scratch, flops, moved):
    return pl.pallas_call(
        body,
        out_shape=out_shape,
        in_specs=in_specs,
        out_specs=out_specs,
        scratch_shapes=scratch,
        compiler_params=pltpu.CompilerParams(vmem_limit_bytes=LIMIT),
        cost_estimate=pl.CostEstimate(flops=flops, bytes_accessed=moved, transcendentals=0),
    )


def sigmoid(values):
    return 0.5 * jnp.tanh(0.5 * values) + 0.5


def dot(left, right, dims):
    return lax.dot_general(left, right, (dims, ((), ())), preferred_element_type=jnp.float32)


def split(values):
    high = values.astype(jnp.bfloat16)
    low = (values - high.astype(jnp.float32)).astype(jnp.bfloat16)
    return jnp.concatenate([high, low], axis=1)


def norm_body(pair_ref, gain_ref, shift_ref, out_ref, held, sems):
    rows, cols, channels = out_ref.shape
    span = lambda at: pl.ds(at * STEP, STEP)
    copies = [
        pltpu.make_async_copy(pair_ref.at[span(at)], held.at[span(at)], sems.at[at])
        for at in range(rows // STEP)
    ]
    for copy in copies:
        copy.start()
    ones = jnp.full((2 * channels, channels), 1.0 / channels, jnp.bfloat16)
    gain, shift = gain_ref[...], shift_ref[...]
    for at, copy in enumerate(copies):
        copy.wait()
        values = held[span(at)].reshape(STEP * cols, channels)
        centered = values - dot(split(values), ones, ((1,), (0,)))
        spread = dot(split(centered * centered), ones, ((1,), (0,)))
        normed = centered * lax.rsqrt(spread + EPS) * gain + shift
        out_ref[span(at)] = normed.astype(jnp.bfloat16).reshape(STEP, cols, channels)


def layer_norm(pair, gain, shift):
    return call(
        norm_body,
        jax.ShapeDtypeStruct(pair.shape, jnp.bfloat16),
        [HBM, VMEM, VMEM],
        VMEM,
        [pltpu.VMEM(pair.shape, jnp.float32), pltpu.SemaphoreType.DMA((pair.shape[0] // STEP,))],
        16 * pair.size,
        6 * pair.size,
    )(pair, gain, shift)


def gate_body(normed_ref, weight_ref, out_ref):
    rows, cols, channels = normed_ref.shape
    weight = weight_ref[...]

    def part(at, carry):
        span = pl.ds(pl.multiple_of(at * STEP, STEP), STEP)
        values = dot(normed_ref[span].reshape(STEP * cols, channels), weight, ((1,), (0,)))
        out_ref[span] = sigmoid(values).reshape(STEP, cols, channels)
        return carry

    lax.fori_loop(0, rows // STEP, part, 0)


def output_gate(normed, weight):
    return call(
        gate_body,
        jax.ShapeDtypeStruct(normed.shape, jnp.float32),
        [VMEM, VMEM],
        VMEM,
        [],
        2 * normed.size * normed.shape[2],
        6 * normed.size,
    )(normed, weight)


def side_body(normed_ref, mask_ref, weight_ref, *rest):
    outs, held = rest[:-1], rest[-1]
    rows, cols, channels = normed_ref.shape
    planes = channels // 2
    weight = weight_ref[...]
    zero = jnp.zeros((cols, channels), jnp.bfloat16)

    def part(at, carry):
        span = pl.ds(pl.multiple_of(at * STEP, STEP), STEP)
        keep = mask_ref[span].astype(jnp.float32)
        keep = jnp.concatenate([keep, keep], axis=1)
        normed = normed_ref[span]
        for row in range(0, STEP, 2):
            parts = []
            for tile in (normed[row], normed[row + 1]):
                parts += [jnp.concatenate([tile, zero], 1), jnp.concatenate([zero, tile], 1)]
            both = dot(weight, jnp.concatenate(parts, axis=0), ((1,), (1,)))
            for more in range(2):
                values = both[:, 2 * cols * more : 2 * cols * (more + 1)]
                kept = values[:planes] * keep[row + more : row + more + 1]
                held[pl.ds(row + more, planes, stride=STEP), :] = sigmoid(values[planes:]) * kept
        done = 0
        for out in outs:
            first = done % planes
            count = out.shape[0]
            value = held[first * STEP : (first + count) * STEP, :]
            out[:, span, :] = value.reshape(count, STEP, 2 * cols).astype(jnp.bfloat16)
            done += count
        return carry

    lax.fori_loop(0, rows // STEP, part, 0)


def side(normed, mask, weight, counts):
    rows, cols, channels = normed.shape
    return call(
        side_body,
        [jax.ShapeDtypeStruct((count, rows, 2 * cols), jnp.bfloat16) for count in counts],
        [VMEM, VMEM, VMEM],
        [VMEM] * len(counts),
        [pltpu.VMEM((channels // 2 * STEP, 2 * cols), jnp.float32)],
        4 * normed.size * channels,
        4 * normed.size,
    )(normed, mask, weight)


def paired(tiles):
    low = lax.broadcasted_iota(jnp.int32, tiles[0].shape, 1) < tiles[0].shape[1] // 2
    zero = jnp.zeros(tiles[0].shape, jnp.bfloat16)
    first = jnp.concatenate([jnp.where(low, tile, zero) for tile in tiles], axis=1)
    second = jnp.concatenate([jnp.where(low, zero, tile) for tile in tiles], axis=1)
    return jnp.concatenate([first, second], axis=0)


def triangle_body(flags_ref, *refs):
    out_ref, count = refs[-1], (len(refs) - 1) // 3
    left, yes, no = refs[:count], refs[count : 2 * count], refs[2 * count : 3 * count]
    flag = flags_ref[0] == 1

    def part(at, carry):
        first = jnp.concatenate([ref[at] for ref in left], axis=1)
        second = paired([jnp.where(flag, one[at], two[at]) for one, two in zip(yes, no)])
        out_ref[at] = dot(first, second, ((1,), (1,))).astype(jnp.bfloat16)
        return carry

    lax.fori_loop(0, out_ref.shape[0], part, 0, unroll=8)


def triangle(flags, left, yes, no):
    planes, rows, lanes = left[0].shape
    return call(
        triangle_body,
        jax.ShapeDtypeStruct((planes, rows, 2 * rows), jnp.bfloat16),
        [SMEM] + [VMEM] * (3 * len(left)),
        VMEM,
        [],
        4 * planes * rows * rows * lanes * len(left),
        6 * left[0].size * len(left),
    )(flags, *left, *yes, *no)


def served_body(start, flags_ref, *refs):
    mine, ends, far, near, outs = (refs[at : at + 2] for at in range(0, 10, 2))
    use_far, swap = flags_ref[0] == 1, flags_ref[1] == 1
    rows = mine[0].shape[1]

    def part(at, carry):
        own = jnp.concatenate([ref[start + at] for ref in mine], axis=1)
        end = jnp.concatenate([ref[start + at] for ref in ends], axis=1)
        first = jnp.concatenate([jnp.where(swap, end, own), jnp.where(swap, own, end)], axis=0)
        second = paired(
            [jnp.where(use_far, one[at], two[start + at]) for one, two in zip(far, near)]
        )
        both = dot(first, second, ((1,), (1,))).astype(jnp.bfloat16)
        outs[0][at] = both[:rows]
        outs[1][at] = both[rows:]
        return carry

    lax.fori_loop(0, outs[0].shape[0], part, 0, unroll=8)


def served(start, flags, mine, ends, far, near):
    count, rows, lanes = far[0].shape
    return call(
        functools.partial(served_body, start),
        [jax.ShapeDtypeStruct((count, rows, 2 * rows), jnp.bfloat16)] * 2,
        [SMEM] + [VMEM] * 8,
        [VMEM] * 2,
        [],
        16 * count * rows * rows * lanes,
        16 * count * rows * lanes,
    )(flags, *mine, *ends, *far, *near)


def finish_body(counts, flags_ref, *refs):
    early, rest = refs[:2], refs[2:]
    chunks = [rest[3 * at : 3 * at + 3] for at in range(len(counts))]
    gain_ref, shift_ref, weight_ref, gate_ref, out_ref = rest[3 * len(counts) :][:5]
    total, held, made, sems = rest[3 * len(counts) + 5 :]
    planes, rows, lanes = early[0].shape
    width = lanes // 2
    is_early, is_middle = flags_ref[2] == 1, flags_ref[3] == 1
    weight = weight_ref[...]

    def mean(values):
        return (values + pltpu.roll(values, width, 1)) * (1.0 / (2 * planes))

    def part(at, carry):
        span = pl.ds(pl.multiple_of(at * STEP, STEP), STEP)
        added = jnp.zeros((STEP, lanes), jnp.float32)
        plane = 0
        for chunk, count in zip(chunks, counts):
            for inner in range(count):
                received, mine, others = (ref[inner, span] for ref in chunk)
                one = jnp.where(is_early, early[0][plane, span], received)
                two = jnp.where(is_middle, mine, others)
                two = jnp.where(is_early, early[1][plane, span], two)
                value = one.astype(jnp.float32) + two.astype(jnp.float32)
                total[plane] = value
                added = added + value
                plane += 1
        middle = mean(added)
        added = jnp.zeros((STEP, lanes), jnp.float32)
        for plane in range(planes):
            centered = total[plane] - middle
            added = added + centered * centered
        scale = lax.rsqrt(mean(added) + EPS)
        for plane in range(planes):
            normed = (total[plane] - middle) * scale * gain_ref[plane] + shift_ref[plane]
            held[pl.ds(plane, STEP, stride=planes), :] = normed
        for row in range(STEP):
            tile = held[row * planes : (row + 1) * planes, :].T.astype(jnp.bfloat16)
            update = dot(tile[:width], weight[:planes], ((1,), (0,)))
            update += dot(tile[width:], weight[planes:], ((1,), (0,)))
            made[at * STEP + row] = update * gate_ref[at * STEP + row]
        pltpu.make_async_copy(made.at[span], out_ref.at[span], sems.at[at]).start()
        return carry

    lax.fori_loop(0, rows // STEP, part, 0)
    for at in range(rows // STEP):
        span = pl.ds(at * STEP, STEP)
        pltpu.make_async_copy(made.at[span], out_ref.at[span], sems.at[at]).wait()


def finish(flags, early, chunks, gain, shift, weight, gate):
    planes, rows, lanes = early[0].shape
    counts = [chunk[0].shape[0] for chunk in chunks]
    parts = [array for chunk in chunks for array in chunk]
    return call(
        functools.partial(finish_body, counts),
        jax.ShapeDtypeStruct(gate.shape, jnp.float32),
        [SMEM] + [VMEM] * (2 + len(parts) + 4),
        HBM,
        [
            pltpu.VMEM((planes, STEP, lanes), jnp.float32),
            pltpu.VMEM((planes * STEP, lanes), jnp.float32),
            pltpu.VMEM(gate.shape, jnp.float32),
            pltpu.SemaphoreType.DMA((rows // STEP,)),
        ],
        2 * gate.size * gate.shape[2],
        8 * gate.size,
    )(flags, *early, *parts, gain, shift, weight, gate)


def planes_of(vector, width):
    return jnp.repeat(vector.reshape(2, -1).T, width, axis=1)[:, None, :]


def per_device(
    mesh_rows,
    mesh_cols,
    pair,
    pair_mask,
    in_gain,
    in_bias,
    proj_weight,
    gate_weight,
    out_gain,
    out_bias,
    out_weight,
):
    rows, cols, channels = pair.shape
    planes = channels // 2
    row, col = lax.axis_index("rows"), lax.axis_index("cols")
    chip, core = col // 2, col % 2

    weights = proj_weight.reshape(channels, 2, 2, 2, planes).transpose(1, 2, 4, 3, 0)
    weights = weights.reshape(2, 2 * planes, 2 * channels)
    gain, shift = planes_of(out_gain, cols), planes_of(out_bias, cols)

    if mesh_rows == 4 and mesh_cols == 4:
        both = ("rows", "cols")
        at = lambda z, x, h: z * 4 + 2 * x + h
        places = [(z, x, h) for z in range(4) for x in range(2) for h in range(2)]
        whole = core == row % 2
        is_early, is_middle = chip == row // 2, (row == 1) | (row == 2)
        flags = jnp.stack([whole, ~is_early, is_early, is_middle]).astype(jnp.int32)
        flip = [(at(z, x, h), at(z, x, 1 - h)) for z, x, h in places]
        to_whole = [(at(z, x, h), at(z, x, 1 - h)) for z, x, h in places if h != z % 2]
        from_whole = [(at(z, x, h), at(z, x, 1 - h)) for z, x, h in places if h == z % 2]
        partners = [(at(z, x, h), at(z ^ 1, x, h)) for z, x, h in places]
        mids = [place for place in places if place[0] in (1, 2)]
        near_straight = [(at(z, x, h), at(3 - z, x, h)) for z, x, h in mids if h == z % 2]
        near_across = [(at(z, x, h), at(3 - z, x, 1 - h)) for z, x, h in mids if h != z % 2]
        far_straight = [(at(z, x, h), at(3 - z, x, h)) for z, x, h in mids if h != z % 2]
        far_across = [(at(z, x, h), at(3 - z, x, 1 - h)) for z, x, h in mids if h == z % 2]
        owner = lambda z: 1 - z // 2
        early_pairs = [(at(z, x, h), at(z, 1 - x, h)) for z, x, h in places if x == owner(z)]
        first_pairs = [(at(z, x, h), at(z ^ 1, x, h)) for z, x, h in mids if x == owner(z)]
        first_pairs += [(at(z, x, h), at(z, 1 - x, h)) for z, x, h in mids if x != owner(z)]
        second_pairs = [(at(z, x, h), at(z ^ 1, 1 - x, h)) for z, x, h in mids if x != owner(z)]
        move = lambda array, pairs: lax.ppermute(array, both, pairs)

        mask_partner = move(pair_mask, partners)
        normed = layer_norm(pair, in_gain[None], in_bias[None])
        normed_partner = move(normed, partners)
        (b_own,) = side(normed, pair_mask, weights[1], [planes])
        near = [move(b_own, near_straight), move(b_own, near_across)]
        b_other = move(b_own, to_whole)
        (a_own,) = side(normed, pair_mask, weights[0], [planes])
        a_other = move(a_own, flip)
        gate = output_gate(normed, gate_weight)
        normed_partner, gate, gain, shift = lax.optimization_barrier(
            (normed_partner, gate, gain, shift)
        )
        count = planes // CHUNKS
        b_partner, *pieces = side(
            normed_partner, mask_partner, weights[1], [planes] + [count] * CHUNKS
        )
        far = [[move(piece, far_straight), move(piece, far_across)] for piece in pieces]
        (a_end,) = side(normed_partner, mask_partner, weights[0], [planes])
        a_end_other = move(a_end, flip)
        b_partner_other = move(b_partner, from_whole)
        product = triangle(
            flags, [a_own, a_other], [b_own, b_other], [b_partner, b_partner_other]
        )
        early = [product, move(product, early_pairs)]
        chunks = []
        for index in range(CHUNKS):
            one, two = served(
                index * count,
                flags,
                [a_own, a_other],
                [a_end, a_end_other],
                far[index],
                near,
            )
            chunks.append([move(one, first_pairs), two, move(two, second_pairs)])
    else:
        flags = jnp.array([1, 0, 1, 0], jnp.int32)
        normed = layer_norm(pair, in_gain[None], in_bias[None])
        count = planes // CHUNKS
        pieces = side(normed, pair_mask, weights[1], [count] * CHUNKS)
        lefts = side(normed, pair_mask, weights[0], [count] * CHUNKS)
        gate = output_gate(normed, gate_weight)
        sums = []
        for piece, left in zip(pieces, lefts):
            gathered = lax.all_gather(piece, "rows")
            blocks = [gathered[index] for index in range(mesh_rows)]
            product = jnp.stack([triangle(flags, [left], [block], [block]) for block in blocks])
            parts = lax.all_to_all(product, "cols", 0, 0, tiled=True)
            sums.append(jnp.sum(parts.astype(jnp.float32), axis=0))
        total = jnp.concatenate(sums, axis=0)
        zero = jnp.zeros_like(total)
        early, chunks = [total, zero], [[total, total, total]]
    return finish(flags, early, chunks, gain, shift, out_weight, gate)


def solution(mesh):
    tile = P(("groups", "rows"), "cols", None)
    return jax.shard_map(
        functools.partial(per_device, mesh.shape["rows"], mesh.shape["cols"]),
        mesh=mesh,
        in_specs=(tile, P(("groups", "rows"), "cols")) + (P(),) * 7,
        out_specs=tile,
        check_vma=False,
    )
```

```python
import functools

import jax
import jax.numpy as jnp
from jax import lax
from jax.experimental import pallas as pl
from jax.experimental.pallas import tpu as pltpu
from jax.sharding import PartitionSpec as P

EPS = 1e-05
VMEM = pl.BlockSpec(memory_space=pltpu.VMEM)
SMEM = pl.BlockSpec(memory_space=pltpu.SMEM)
HBM = pl.BlockSpec(memory_space=pltpu.HBM)
STEP = 16


def call(body, out_shape, in_specs, out_specs, scratch, limit=12):
    return pl.pallas_call(
        body,
        out_shape=out_shape,
        in_specs=in_specs,
        out_specs=out_specs,
        scratch_shapes=scratch,
        compiler_params=pltpu.CompilerParams(vmem_limit_bytes=limit * 1024 * 1024),
        cost_estimate=pl.CostEstimate(flops=1, bytes_accessed=1, transcendentals=0),
    )


def sigmoid(values):
    return 0.5 * jnp.tanh(0.5 * values) + 0.5


def dot(left, right, dims):
    return lax.dot_general(left, right, (dims, ((), ())), preferred_element_type=jnp.float32)


def split(values):
    high = values.astype(jnp.bfloat16)
    low = (values - high.astype(jnp.float32)).astype(jnp.bfloat16)
    return jnp.concatenate([high, low], axis=1)


def norm_body(pair_ref, mask_ref, gain_ref, shift_ref, *refs):
    out_ref, kept_ref, held, mask, gain_held, shift_held, sems = refs
    rows, cols, channels = out_ref.shape
    steps = rows // STEP
    span = lambda at: pl.ds(at * STEP, STEP)
    small = [
        pltpu.make_async_copy(mask_ref, mask, sems.at[steps]),
        pltpu.make_async_copy(gain_ref, gain_held, sems.at[steps + 1]),
        pltpu.make_async_copy(shift_ref, shift_held, sems.at[steps + 2]),
    ]
    copies = [
        pltpu.make_async_copy(pair_ref.at[span(at)], held.at[span(at)], sems.at[at])
        for at in range(steps)
    ]
    for copy in copies[:1] + small + copies[1:]:
        copy.start()
    ones = jnp.full((2 * channels, channels), 1.0 / channels, jnp.bfloat16)
    for copy in small:
        copy.wait()
    gain, shift = gain_held[...], shift_held[...]
    for at, copy in enumerate(copies):
        copy.wait()
        values = held[span(at)].reshape(STEP * cols, channels)
        centered = values - dot(split(values), ones, ((1,), (0,)))
        squares = (centered * centered).astype(jnp.bfloat16)
        spread = dot(squares, ones[:channels], ((1,), (0,)))
        normed = centered * lax.rsqrt(spread + EPS) * gain + shift
        out_ref[span(at)] = normed.astype(jnp.bfloat16).reshape(STEP, cols, channels)
        keep = mask[span(at)].astype(jnp.float32).T
        for row in range(STEP):
            tile = normed[row * cols : (row + 1) * cols] * keep[:, row : row + 1]
            kept_ref[at * STEP + row] = tile.astype(jnp.bfloat16)


def layer_norm(pair, mask, gain, shift):
    return call(
        norm_body,
        [jax.ShapeDtypeStruct(pair.shape, jnp.bfloat16)] * 2,
        [HBM] * 4,
        [VMEM] * 2,
        [
            pltpu.VMEM(pair.shape, jnp.float32),
            pltpu.VMEM(mask.shape, jnp.int32),
            pltpu.VMEM(gain.shape, jnp.float32),
            pltpu.VMEM(shift.shape, jnp.float32),
            pltpu.SemaphoreType.DMA((pair.shape[0] // STEP + 3,)),
        ],
        limit=58,
    )(pair, mask, gain, shift)


def gate_body(normed_ref, weight_ref, out_ref, held, sems):
    rows, cols, channels = normed_ref.shape
    weight = weight_ref[...]
    copies = []
    for at in range(rows // STEP):
        span = pl.ds(at * STEP, STEP)
        values = dot(normed_ref[span].reshape(STEP * cols, channels), weight, ((1,), (0,)))
        held[span] = sigmoid(values).reshape(STEP, cols, channels)
        copies.append(pltpu.make_async_copy(held.at[span], out_ref.at[span], sems.at[at]))
        copies[-1].start()
    for copy in copies:
        copy.wait()


def output_gate(normed, weight):
    return call(
        gate_body,
        jax.ShapeDtypeStruct(normed.shape, jnp.float32),
        [VMEM, VMEM],
        HBM,
        [
            pltpu.VMEM(normed.shape, jnp.float32),
            pltpu.SemaphoreType.DMA((normed.shape[0] // STEP,)),
        ],
    )(normed, weight)


def side_body(cases, flags_ref, weight_ref, *refs):
    tiles, outs, held = refs[: -1 - len(cases[0][1])], refs[-1 - len(cases[0][1]) : -1], refs[-1]
    rows, cols, channels = tiles[0].shape
    planes = channels // 2
    zero = jnp.zeros((cols, channels), jnp.bfloat16)

    def project(tile_ref, first, out_ref):
        count = out_ref.shape[0]
        weight = jnp.concatenate(
            [weight_ref[first : first + count], weight_ref[planes + first : planes + first + count]], axis=0
        )

        def part(at, carry):
            span = pl.ds(pl.multiple_of(at * STEP, STEP), STEP)
            normed = tile_ref[span]
            for row in range(0, STEP, 2):
                parts = []
                for tile in (normed[row], normed[row + 1]):
                    parts += [jnp.concatenate([tile, zero], 1), jnp.concatenate([zero, tile], 1)]
                both = dot(weight, jnp.concatenate(parts, axis=0), ((1,), (1,)))
                for more in range(2):
                    values = both[:, 2 * cols * more : 2 * cols * (more + 1)]
                    held[pl.ds(row + more, count, stride=STEP), :] = (
                        sigmoid(values[count:]) * values[:count]
                    )
            value = held[: count * STEP, :].reshape(count, STEP, 2 * cols)
            out_ref[:, span, :] = value.astype(jnp.bfloat16)
            return carry

        lax.fori_loop(0, rows // STEP, part, 0)

    def work(jobs):
        for tile, first, out, index in jobs:
            project(tiles[tile], first, outs[out] if index is None else outs[out].at[index])

    if len(cases) == 1:
        work(cases[0][0])
    else:
        for value, (jobs, _) in enumerate(cases):
            pl.when(flags_ref[0] == value)(functools.partial(work, jobs))


def side(cases, shapes, flags, weight, tiles):
    cases = [(jobs, shapes) for jobs in cases]
    rows, cols, channels = tiles[0].shape
    return call(
        functools.partial(side_body, cases),
        [jax.ShapeDtypeStruct(shape + (rows, 2 * cols), jnp.bfloat16) for shape in shapes],
        [SMEM] + [VMEM] * (1 + len(tiles)),
        [VMEM] * len(shapes),
        [pltpu.VMEM((channels // 2 * STEP, 2 * cols), jnp.float32)],
    )(flags, weight, *tiles)


def paired(tiles):
    low = lax.broadcasted_iota(jnp.int32, tiles[0].shape, 1) < tiles[0].shape[1] // 2
    zero = jnp.zeros(tiles[0].shape, jnp.bfloat16)
    first = jnp.concatenate([jnp.where(low, tile, zero) for tile in tiles], axis=1)
    second = jnp.concatenate([jnp.where(low, zero, tile) for tile in tiles], axis=1)
    return jnp.concatenate([first, second], axis=0)


def triangle_body(cases, flags_ref, *refs):
    left, right, out_ref = refs[:2], refs[2:-1], refs[-1]

    def work(places):
        for plane, place in enumerate(places):
            first = jnp.concatenate([ref[plane] for ref in left], axis=1)
            second = paired([right[at[0]][at[1:]] for at in place])
            value = dot(first, second, ((1,), (1,)))
            out_ref[plane] = value.astype(jnp.bfloat16)

    for case, places in enumerate(cases):
        pl.when(flags_ref[0] == case)(functools.partial(work, places))


def triangle(cases, flags, left, right):
    planes, rows, lanes = left[0].shape
    return call(
        functools.partial(triangle_body, cases),
        jax.ShapeDtypeStruct((planes, rows, 2 * rows), jnp.bfloat16),
        [SMEM] + [VMEM] * (2 + len(right)),
        VMEM,
        [],
    )(flags, *left, *right)


def served_body(which, start, flags_ref, *refs):
    mine, ends, right, outs = refs[:2], refs[2:4], refs[4:-2], refs[-2:]
    rows = mine[0].shape[1]
    tiles = right if len(right) == 2 else [right[0].at[0], right[0].at[1]]

    def work(firsts):
        for at in range(outs[0].shape[0]):
            both = [
                jnp.concatenate([ref[start + at] for ref in first], axis=1) for first in firsts
            ]
            second = paired([ref[at] for ref in tiles])
            value = dot(jnp.concatenate(both, axis=0), second, ((1,), (1,)))
            value = value.astype(jnp.bfloat16)
            outs[0][at] = value[:rows]
            outs[1][at] = value[rows:]

    @pl.when((flags_ref[0] == which) & (flags_ref[1] == 1))
    def _():
        work([ends, mine])

    @pl.when((flags_ref[0] == which) & (flags_ref[1] == 0))
    def _():
        work([mine, ends])


def served(which, start, flags, mine, ends, right):
    count, rows, lanes = right[0].shape[-3:]
    return call(
        functools.partial(served_body, which, start),
        [jax.ShapeDtypeStruct((count, rows, 2 * rows), jnp.bfloat16)] * 2,
        [SMEM] + [VMEM] * (4 + len(right)),
        [VMEM] * 2,
        [],
    )(flags, *mine, *ends, *right)


def finish_body(cases, flags_ref, *refs):
    parts, (gain_ref, shift_ref, weight_ref, gate_ref, out_ref) = refs[:-10], refs[-10:-5]
    total, held, made, gate, sems = refs[-5:]
    planes, _, lanes = total.shape
    rows = gate.shape[0]
    steps = rows // STEP
    width = lanes // 2
    weight = weight_ref[...]
    spans = [pl.ds(at * STEP, STEP) for at in range(steps)]
    loads = [
        pltpu.make_async_copy(gate_ref.at[span], gate.at[span], sems.at[at])
        for at, span in enumerate(spans)
    ]
    for load in loads:
        load.start()

    def mean(values):
        return (values + pltpu.roll(values, width, 1)) * (1.0 / (2 * planes))

    def part(at, carry):
        span = pl.ds(pl.multiple_of(at * STEP, STEP), STEP)
        for case, (first, second) in enumerate(cases):

            @pl.when(flags_ref[2] == case)
            def _():
                ones = [(index, at) for index in first for at in range(parts[index].shape[0])]
                twos = [(index, at) for index in second for at in range(parts[index].shape[0])]
                for plane in range(planes):
                    (one, here), (two, there) = ones[plane], twos[plane]
                    value = parts[one][here, span].astype(jnp.float32)
                    total[plane] = value + parts[two][there, span].astype(jnp.float32)

        added = jnp.zeros((STEP, lanes), jnp.float32)
        for plane in range(planes):
            added = added + total[plane]
        middle = mean(added)
        added = jnp.zeros((STEP, lanes), jnp.float32)
        for plane in range(planes):
            centered = total[plane] - middle
            added = added + centered * centered
        scale = lax.rsqrt(mean(added) + EPS)
        for plane in range(planes):
            normed = (total[plane] - middle) * scale * gain_ref[plane] + shift_ref[plane]
            held[pl.ds(plane, STEP, stride=planes), :] = normed
        pltpu.make_async_copy(gate_ref.at[span], gate.at[span], sems.at[at]).wait()
        for row in range(STEP):
            tile = held[row * planes : (row + 1) * planes, :].T.astype(jnp.bfloat16)
            update = dot(tile[:width], weight[:planes], ((1,), (0,)))
            update += dot(tile[width:], weight[planes:], ((1,), (0,)))
            made[at * STEP + row] = update * gate[at * STEP + row]
        pltpu.make_async_copy(made.at[span], out_ref.at[span], sems.at[steps + at]).start()
        return carry

    lax.fori_loop(0, steps, part, 0)
    for at, span in enumerate(spans):
        pltpu.make_async_copy(made.at[span], out_ref.at[span], sems.at[steps + at]).wait()


def finish(flags, cases, parts, gain, shift, weight, gate):
    planes, _, lanes = gain.shape
    rows = gate.shape[0]
    return call(
        functools.partial(finish_body, cases),
        jax.ShapeDtypeStruct(gate.shape, jnp.float32),
        [SMEM] + [VMEM] * (len(parts) + 3) + [HBM],
        HBM,
        [
            pltpu.VMEM((planes, STEP, lanes), jnp.float32),
            pltpu.VMEM((planes * STEP, lanes), jnp.float32),
            pltpu.VMEM(gate.shape, jnp.float32),
            pltpu.VMEM(gate.shape, jnp.float32),
            pltpu.SemaphoreType.DMA((2 * rows // STEP,)),
        ],
    )(flags, *parts, gain, shift, weight, gate)


def planes_of(vector, width):
    return jnp.repeat(vector.reshape(2, -1).T, width, axis=1)[:, None, :]


def arranged(weight):
    channels = weight.shape[0]
    weight = weight.reshape(channels, 2, 2, 2, channels // 2).transpose(1, 2, 4, 3, 0)
    return weight.reshape(2, channels, 2 * channels)


def per_device(
    mesh_rows,
    mesh_cols,
    pair,
    pair_mask,
    in_gain,
    in_bias,
    proj_weight,
    gate_weight,
    out_gain,
    out_bias,
    out_weight,
):
    rows, cols, channels = pair.shape
    planes = channels // 2
    row, col = lax.axis_index("rows"), lax.axis_index("cols")
    chip, core = col // 2, col % 2

    gain, shift = planes_of(out_gain, cols), planes_of(out_bias, cols)

    if mesh_rows == 4 and mesh_cols == 4:
        both = ("rows", "cols")
        at = lambda z, x, h: z * 4 + 2 * x + h
        places = [(z, x, h) for z in range(4) for x in range(2) for h in range(2)]
        whole = core == row % 2
        is_early, is_middle = chip == row // 2, (row == 1) | (row == 2)
        late = jnp.where(is_middle, 1, 2) + jnp.where(whole == is_middle, 0, 2)
        case = jnp.where(is_early, 0, late)
        flags = jnp.stack([whole, ~is_early, case]).astype(jnp.int32)
        flip = [(at(z, x, h), at(z, x, 1 - h)) for z, x, h in places]
        wholes = [place for place in places if place[2] == place[0] % 2]
        others = [place for place in places if place[2] != place[0] % 2]
        partners = [(at(z, x, h), at(z ^ 1, x, h)) for z, x, h in places]
        swap = lambda some: [(at(z, x, h), at(z, x, 1 - h)) for z, x, h in some]
        middles = lambda some: [place for place in some if place[0] in (1, 2)]
        straight = lambda some: [(at(z, x, h), at(3 - z, x, h)) for z, x, h in middles(some)]
        diagonal = lambda some: [(at(z, x, h), at(3 - z, x, 1 - h)) for z, x, h in middles(some)]
        owner = lambda z: 1 - z // 2
        early_pairs = [(at(z, x, h), at(z, 1 - x, h)) for z, x, h in places if x == owner(z)]
        first_pairs = lambda some: [
            (at(z, x, h), at(z ^ 1, x, h) if x == owner(z) else at(z, 1 - x, h))
            for z, x, h in middles(some)
        ]
        second_pairs = lambda some: [
            (at(z, x, h), at(z ^ 1, 1 - x, h)) for z, x, h in middles(some) if x != owner(z)
        ]
        move = lambda array, pairs: lax.ppermute(array, both, pairs)
        tie = lax.optimization_barrier
        full = [[(0, 0, 0, None)]]
        side_of = lambda column, tile: side(full, [(planes,)], flags, weights[column], [tile])

        normed, kept = layer_norm(pair, pair_mask, in_gain[None], in_bias[None])
        kept_partner = move(kept, partners)
        kept_other = move(kept, flip)
        kept, proj_weight = tie((kept, proj_weight))
        weights = arranged(proj_weight)
        (b_own,) = side_of(1, kept)
        near = [move(b_own, straight(wholes)), move(b_own, diagonal(others))]
        kept, b_own = tie((kept, b_own))
        (a_own,) = side_of(0, kept)
        (a_other,) = side_of(0, kept_other)
        (b_other,) = side([[], full[0]], [(planes,)], flags, weights[1], [kept_other])
        gate = output_gate(normed, gate_weight)
        kept_partner, a_own, a_other, b_other, gate, gain, shift = tie(
            (kept_partner, a_own, a_other, b_other, gate, gain, shift)
        )
        kept_partner_other = move(kept_partner, flip)
        (b_partner,) = side_of(1, kept_partner)
        far = [move(b_partner, straight(others)), move(b_partner, diagonal(wholes))]
        b_partner_other = move(b_partner, swap(wholes))
        kept_partner, b_partner, near = tie((kept_partner, b_partner, near))
        (a_end,) = side_of(0, kept_partner)
        kept_partner_other, a_end = tie((kept_partner_other, a_end))
        (a_end_other,) = side_of(0, kept_partner_other)
        b_partner, a_end, a_end_other = tie((b_partner, a_end, a_end_other))
        mine, ends = [a_own, a_other], [a_end, a_end_other]
        cases = [
            [[(2 * case + tile, plane) for tile in (0, 1)] for plane in range(planes)]
            for case in (0, 1)
        ]
        early = triangle(cases, flags, mine, [b_partner, b_partner_other, b_own, b_other])
        early_other = move(early, early_pairs)
        near, early = tie((near, early))
        parts = [early, early_other]
        one, two = served(0, 0, flags, mine, ends, near)
        parts += [move(one, first_pairs(others)), two, move(two, second_pairs(others))]
        far, parts = tie((far, parts[:1] + parts[2:])), [parts[1]]
        far, parts = far[0], far[1][:1] + parts + far[1][1:]
        one, two = served(1, 0, flags, mine, ends, far)
        parts += [move(one, first_pairs(wholes)), two, move(two, second_pairs(wholes))]
        cases = [([0], [1]), ([5], [6]), ([5], [7]), ([2], [3]), ([2], [4])]
    else:
        flags = jnp.zeros((3,), jnp.int32)
        normed, kept = layer_norm(pair, pair_mask, in_gain[None], in_bias[None])
        quarters = [[(0, planes // 4 * at, at, None) for at in range(4)]]
        shapes = [(planes // 4,)] * 4
        weights = arranged(proj_weight)
        pieces = side(quarters, shapes, flags, weights[1], [kept])
        lefts = side(quarters, shapes, flags, weights[0], [kept])
        gate = output_gate(normed, gate_weight)
        places = [[[(0, plane), (1, plane)] for plane in range(planes // 4)]]
        sums = []
        for piece, left in zip(pieces, lefts):
            gathered = lax.all_gather(piece, "rows")
            zero = jnp.zeros_like(left)
            product = jnp.stack(
                [
                    triangle(places, flags, [left, zero], [gathered[at], zero])
                    for at in range(mesh_rows)
                ]
            )
            gathered = lax.all_to_all(product, "cols", 0, 0, tiled=True)
            sums.append(jnp.sum(gathered.astype(jnp.float32), axis=0))
        total = jnp.concatenate(sums, axis=0)
        parts, cases = [total, jnp.zeros_like(total)], [([0], [1])]
    return finish(flags, cases, parts, gain, shift, out_weight, gate)


def solution(mesh):
    tile = P(("groups", "rows"), "cols", None)
    return jax.shard_map(
        functools.partial(per_device, mesh.shape["rows"], mesh.shape["cols"]),
        mesh=mesh,
        in_specs=(tile, P(("groups", "rows"), "cols")) + (P(),) * 7,
        out_specs=tile,
        check_vma=False,
    )
```

```python
import functools

import jax
import jax.numpy as jnp
from jax import lax
from jax.experimental import pallas as pl
from jax.experimental.pallas import tpu as pltpu
from jax.sharding import PartitionSpec as P

EPS = 1e-05
VMEM = pl.BlockSpec(memory_space=pltpu.VMEM)
HBM = pl.BlockSpec(memory_space=pltpu.HBM)
STEP = 16


def place():
    row, col = lax.axis_index("rows"), lax.axis_index("cols")
    whole = col % 2 == row % 2
    early, middle = col // 2 == row // 2, (row == 1) | (row == 2)
    late = jnp.where(middle, 1, 2) + jnp.where(whole == middle, 0, 2)
    return whole.astype(jnp.int32), ~early, jnp.where(early, 0, late)


def call(body, out_shape, in_specs, out_specs, scratch, limit=12):
    return pl.pallas_call(
        body,
        out_shape=out_shape,
        in_specs=in_specs,
        out_specs=out_specs,
        scratch_shapes=scratch,
        compiler_params=pltpu.CompilerParams(vmem_limit_bytes=limit * 1024 * 1024),
        cost_estimate=pl.CostEstimate(flops=1, bytes_accessed=1, transcendentals=0),
    )


def sigmoid(values):
    return 0.5 * jnp.tanh(0.5 * values) + 0.5


def dot(left, right, dims):
    return lax.dot_general(left, right, (dims, ((), ())), preferred_element_type=jnp.float32)


def split(values):
    high = values.astype(jnp.bfloat16)
    low = (values - high.astype(jnp.float32)).astype(jnp.bfloat16)
    return jnp.concatenate([high, low], axis=1)


def norm_body(pair_ref, mask_ref, gain_ref, shift_ref, *refs):
    out_ref, kept_ref, held, mask, gain_held, shift_held, sems = refs
    rows, cols, channels = out_ref.shape
    steps = rows // STEP
    span = lambda at: pl.ds(at * STEP, STEP)
    small = [
        pltpu.make_async_copy(mask_ref, mask, sems.at[steps]),
        pltpu.make_async_copy(gain_ref, gain_held, sems.at[steps + 1]),
        pltpu.make_async_copy(shift_ref, shift_held, sems.at[steps + 2]),
    ]
    copies = [
        pltpu.make_async_copy(pair_ref.at[span(at)], held.at[span(at)], sems.at[at])
        for at in range(steps)
    ]
    for copy in copies[:1] + small + copies[1:]:
        copy.start()
    ones = jnp.full((2 * channels, channels), 1.0 / channels, jnp.bfloat16)
    for copy in small:
        copy.wait()
    gain, shift = gain_held[...], shift_held[...]
    for at, copy in enumerate(copies):
        copy.wait()
        values = held[span(at)].reshape(STEP * cols, channels)
        centered = values - dot(split(values), ones, ((1,), (0,)))
        squares = (centered * centered).astype(jnp.bfloat16)
        spread = dot(squares, ones[:channels], ((1,), (0,)))
        normed = centered * lax.rsqrt(spread + EPS) * gain + shift
        out_ref[span(at)] = normed.astype(jnp.bfloat16).reshape(STEP, cols, channels)
        keep = mask[span(at)].astype(jnp.float32).T
        for row in range(STEP):
            tile = normed[row * cols : (row + 1) * cols] * keep[:, row : row + 1]
            kept_ref[at * STEP + row] = tile.astype(jnp.bfloat16)


def layer_norm(pair, mask, gain, shift):
    return call(
        norm_body,
        [jax.ShapeDtypeStruct(pair.shape, jnp.bfloat16)] * 2,
        [HBM] * 4,
        [VMEM] * 2,
        [
            pltpu.VMEM(pair.shape, jnp.float32),
            pltpu.VMEM(mask.shape, jnp.int32),
            pltpu.VMEM(gain.shape, jnp.float32),
            pltpu.VMEM(shift.shape, jnp.float32),
            pltpu.SemaphoreType.DMA((pair.shape[0] // STEP + 3,)),
        ],
        limit=58,
    )(pair, mask, gain, shift)


def gate_body(normed_ref, weight_ref, out_ref, held, sems):
    rows, cols, channels = normed_ref.shape
    weight = weight_ref[...]
    copies = []
    for at in range(rows // STEP):
        span = pl.ds(at * STEP, STEP)
        values = dot(normed_ref[span].reshape(STEP * cols, channels), weight, ((1,), (0,)))
        held[span] = sigmoid(values).reshape(STEP, cols, channels)
        copies.append(pltpu.make_async_copy(held.at[span], out_ref.at[span], sems.at[at]))
        copies[-1].start()
    for copy in copies:
        copy.wait()


def output_gate(normed, weight):
    return call(
        gate_body,
        jax.ShapeDtypeStruct(normed.shape, jnp.float32),
        [VMEM, VMEM],
        HBM,
        [
            pltpu.VMEM(normed.shape, jnp.float32),
            pltpu.SemaphoreType.DMA((normed.shape[0] // STEP,)),
        ],
    )(normed, weight)


def side_body(cases, weight_ref, *refs):
    tiles, outs, held = refs[: -1 - len(cases[0][1])], refs[-1 - len(cases[0][1]) : -1], refs[-1]
    rows, cols, channels = tiles[0].shape
    planes = channels // 2
    zero = jnp.zeros((cols, channels), jnp.bfloat16)

    def project(tile_ref, first, out_ref):
        count = out_ref.shape[0]
        weight = jnp.concatenate(
            [weight_ref[first : first + count], weight_ref[planes + first : planes + first + count]], axis=0
        )

        def part(at, carry):
            span = pl.ds(pl.multiple_of(at * STEP, STEP), STEP)
            normed = tile_ref[span]
            for row in range(0, STEP, 2):
                parts = []
                for tile in (normed[row], normed[row + 1]):
                    parts += [jnp.concatenate([tile, zero], 1), jnp.concatenate([zero, tile], 1)]
                both = dot(weight, jnp.concatenate(parts, axis=0), ((1,), (1,)))
                for more in range(2):
                    values = both[:, 2 * cols * more : 2 * cols * (more + 1)]
                    held[pl.ds(row + more, count, stride=STEP), :] = (
                        sigmoid(values[count:]) * values[:count]
                    )
            value = held[: count * STEP, :].reshape(count, STEP, 2 * cols)
            out_ref[:, span, :] = value.astype(jnp.bfloat16)
            return carry

        lax.fori_loop(0, rows // STEP, part, 0, unroll=True)

    def work(jobs):
        for tile, first, out, index in jobs:
            project(tiles[tile], first, outs[out] if index is None else outs[out].at[index])

    if len(cases) == 1:
        work(cases[0][0])
    else:
        whole = place()[0]
        for value, (jobs, _) in enumerate(cases):
            pl.when(whole == value)(functools.partial(work, jobs))


def side(cases, shapes, weight, tiles):
    cases = [(jobs, shapes) for jobs in cases]
    rows, cols, channels = tiles[0].shape
    return call(
        functools.partial(side_body, cases),
        [jax.ShapeDtypeStruct(shape + (rows, 2 * cols), jnp.bfloat16) for shape in shapes],
        [VMEM] * (1 + len(tiles)),
        [VMEM] * len(shapes),
        [pltpu.VMEM((channels // 2 * STEP, 2 * cols), jnp.float32)],
    )(weight, *tiles)


def paired(tiles):
    low = lax.broadcasted_iota(jnp.int32, tiles[0].shape, 1) < tiles[0].shape[1] // 2
    zero = jnp.zeros(tiles[0].shape, jnp.bfloat16)
    first = jnp.concatenate([jnp.where(low, tile, zero) for tile in tiles], axis=1)
    second = jnp.concatenate([jnp.where(low, zero, tile) for tile in tiles], axis=1)
    return jnp.concatenate([first, second], axis=0)


def triangle_body(cases, *refs):
    left, right, out_ref = refs[:2], refs[2:-1], refs[-1]

    def work(places):
        for plane, place in enumerate(places):
            first = jnp.concatenate([ref[plane] for ref in left], axis=1)
            second = paired([right[at[0]][at[1:]] for at in place])
            value = dot(first, second, ((1,), (1,)))
            out_ref[plane] = value.astype(jnp.bfloat16)

    if len(cases) == 1:
        work(cases[0])
    else:
        whole = place()[0]
        for case, places in enumerate(cases):
            pl.when(whole == case)(functools.partial(work, places))


def triangle(cases, left, right):
    planes, rows, lanes = left[0].shape
    return call(
        functools.partial(triangle_body, cases),
        jax.ShapeDtypeStruct((planes, rows, 2 * rows), jnp.bfloat16),
        [VMEM] * (2 + len(right)),
        VMEM,
        [],
    )(*left, *right)


def served_body(which, mine_ref, other_ref, ends_ref, right_ref, *outs):
    mine, ends = [mine_ref, other_ref], [ends_ref.at[which], ends_ref.at[1 - which]]
    rows = mine_ref.shape[1]

    def work(firsts):
        for at in range(outs[0].shape[0]):
            both = [jnp.concatenate([ref[at] for ref in first], axis=1) for first in firsts]
            second = paired([right_ref[0, at], right_ref[1, at]])
            value = dot(jnp.concatenate(both, axis=0), second, ((1,), (1,)))
            value = value.astype(jnp.bfloat16)
            outs[0][at] = value[:rows]
            outs[1][at] = value[rows:]

    whole, owner, _ = place()

    @pl.when((whole == which) & owner)
    def _():
        work([ends, mine])

    @pl.when((whole == which) & ~owner)
    def _():
        work([mine, ends])


def served(which, mine, ends, right):
    planes, rows, _ = mine[0].shape
    return call(
        functools.partial(served_body, which),
        [jax.ShapeDtypeStruct((planes, rows, 2 * rows), jnp.bfloat16)] * 2,
        [VMEM] * 4,
        [VMEM] * 2,
        [],
    )(*mine, ends, right)


def finish_body(cases, *refs):
    parts, (gain_ref, shift_ref, weight_ref, gate_ref, out_ref) = refs[:-10], refs[-10:-5]
    total, held, made, gate, sems = refs[-5:]
    planes, _, lanes = total.shape
    rows = gate.shape[0]
    steps = rows // STEP
    width = lanes // 2
    weight = weight_ref[...]
    spans = [pl.ds(at * STEP, STEP) for at in range(steps)]
    mine = place()[2] if len(cases) > 1 else 0
    loads = [
        pltpu.make_async_copy(gate_ref.at[span], gate.at[span], sems.at[at])
        for at, span in enumerate(spans)
    ]
    for load in loads:
        load.start()

    def mean(values):
        return (values + pltpu.roll(values, width, 1)) * (1.0 / (2 * planes))

    def part(at, carry):
        span = pl.ds(pl.multiple_of(at * STEP, STEP), STEP)
        for case, (first, second) in enumerate(cases):

            @pl.when(mine == case)
            def _():
                ones = [(index, at) for index in first for at in range(parts[index].shape[0])]
                twos = [(index, at) for index in second for at in range(parts[index].shape[0])]
                for plane in range(planes):
                    (one, here), (two, there) = ones[plane], twos[plane]
                    value = parts[one][here, span].astype(jnp.float32)
                    total[plane] = value + parts[two][there, span].astype(jnp.float32)

        added = jnp.zeros((STEP, lanes), jnp.float32)
        for plane in range(planes):
            added = added + total[plane]
        middle = mean(added)
        added = jnp.zeros((STEP, lanes), jnp.float32)
        for plane in range(planes):
            centered = total[plane] - middle
            added = added + centered * centered
        scale = lax.rsqrt(mean(added) + EPS)
        for plane in range(planes):
            normed = (total[plane] - middle) * scale * gain_ref[plane] + shift_ref[plane]
            held[pl.ds(plane, STEP, stride=planes), :] = normed
        pltpu.make_async_copy(gate_ref.at[span], gate.at[span], sems.at[at]).wait()
        for row in range(STEP):
            tile = held[row * planes : (row + 1) * planes, :].T.astype(jnp.bfloat16)
            update = dot(tile[:width], weight[:planes], ((1,), (0,)))
            update += dot(tile[width:], weight[planes:], ((1,), (0,)))
            made[at * STEP + row] = update * gate[at * STEP + row]
        pltpu.make_async_copy(made.at[span], out_ref.at[span], sems.at[steps + at]).start()
        return carry

    lax.fori_loop(0, steps, part, 0)
    for at, span in enumerate(spans):
        pltpu.make_async_copy(made.at[span], out_ref.at[span], sems.at[steps + at]).wait()


def finish(cases, parts, gain, shift, weight, gate):
    planes, _, lanes = gain.shape
    rows = gate.shape[0]
    return call(
        functools.partial(finish_body, cases),
        jax.ShapeDtypeStruct(gate.shape, jnp.float32),
        [VMEM] * (len(parts) + 3) + [HBM],
        HBM,
        [
            pltpu.VMEM((planes, STEP, lanes), jnp.float32),
            pltpu.VMEM((planes * STEP, lanes), jnp.float32),
            pltpu.VMEM(gate.shape, jnp.float32),
            pltpu.VMEM(gate.shape, jnp.float32),
            pltpu.SemaphoreType.DMA((2 * rows // STEP,)),
        ],
    )(*parts, gain, shift, weight, gate)


def planes_of(vector, width):
    return jnp.repeat(vector.reshape(2, -1).T, width, axis=1)[:, None, :]


def arranged(weight):
    channels = weight.shape[0]
    weight = weight.reshape(channels, 2, 2, 2, channels // 2).transpose(1, 2, 4, 3, 0)
    return weight.reshape(2, channels, 2 * channels)


def per_device(
    mesh_rows,
    mesh_cols,
    pair,
    pair_mask,
    in_gain,
    in_bias,
    proj_weight,
    gate_weight,
    out_gain,
    out_bias,
    out_weight,
):
    rows, cols, channels = pair.shape
    planes = channels // 2
    gain, shift = planes_of(out_gain, cols), planes_of(out_bias, cols)

    if mesh_rows == 4 and mesh_cols == 4:
        both = ("rows", "cols")
        at = lambda z, x, h: z * 4 + 2 * x + h
        places = [(z, x, h) for z in range(4) for x in range(2) for h in range(2)]
        flip = [(at(z, x, h), at(z, x, 1 - h)) for z, x, h in places]
        wholes = [place for place in places if place[2] == place[0] % 2]
        others = [place for place in places if place[2] != place[0] % 2]
        middles = lambda some: [place for place in some if place[0] in (1, 2)]
        partners = [(at(z, x, h), at(z ^ 1, x, h)) for z, x, h in wholes]
        from_others = [(at(z, x, h), at(z, x, 1 - h)) for z, x, h in others]
        straight = [(at(z, x, h), at(3 - z, x, h)) for z, x, h in middles(wholes)]
        diagonal = [(at(z, x, h), at(3 - z, x, 1 - h)) for z, x, h in middles(others)]
        two_hops = [(at(z, x, h), at(2 - z // 3, x, h)) for z, x, h in wholes if z in (0, 3)]
        owner = lambda z: 1 - z // 2
        early_pairs = [(at(z, x, h), at(z, 1 - x, h)) for z, x, h in places if x == owner(z)]
        first_pairs = lambda some: [
            (at(z, x, h), at(z ^ 1, x, h) if x == owner(z) else at(z, 1 - x, h))
            for z, x, h in middles(some)
        ]
        second_pairs = lambda some: [
            (at(z, x, h), at(z ^ 1, 1 - x, h)) for z, x, h in middles(some) if x != owner(z)
        ]
        move = lambda array, pairs: lax.ppermute(array, both, pairs)
        tie = lax.optimization_barrier
        full = [[(0, 0, 0, None)]]
        side_of = lambda column, tile: side(full, [(planes,)], weights[column], [tile])

        normed, kept = layer_norm(pair, pair_mask, in_gain[None], in_bias[None])
        kept_other = move(kept, flip)
        near = [move(kept, straight), move(kept, diagonal)]
        partner = move(kept, partners)
        partner_other = move(kept_other, partners)
        kept, proj_weight = tie((kept, proj_weight))
        weights = arranged(proj_weight)
        tiles = [(0, 0, 0, 0), (1, 0, 0, 1)]
        both_tiles = [(2, planes)]
        (b_own,) = side([[], tiles], both_tiles, weights[1], [kept, kept_other])
        kept, b_own = tie((kept, b_own))
        (a_own,) = side_of(0, kept)
        (a_other,) = side_of(0, kept_other)
        gate = output_gate(normed, gate_weight)
        near, a_own, a_other, b_own, gate, gain, shift = tie(
            (near, a_own, a_other, b_own, gate, gain, shift)
        )
        far = move(b_own, two_hops)
        partner, near = tie((partner, near))
        (b_near,) = side([tiles, []], both_tiles, weights[1], near)
        partner_other, partner, b_near = tie((partner_other, partner, b_near))
        (a_end,) = side([tiles, []], both_tiles, weights[0], [partner, partner_other])
        a_end_moved = move(a_end, from_others)
        mine = [a_own, a_other]
        one, two = served(0, mine, a_end, b_near)
        near = [move(one, first_pairs(others)), two, move(two, second_pairs(others))]
        partner_other, one = tie((partner_other, one))
        (b_partner,) = side([tiles, []], both_tiles, weights[1], [partner, partner_other])
        cases = [[[(case, 0, at), (case, 1, at)] for at in range(planes)] for case in (0, 1)]
        early = triangle(cases, mine, [b_partner, b_own])
        early_other = move(early, early_pairs)
        far, near, early = tie((far, near, early))
        a_end_moved, far = tie((a_end_moved, far))
        one, two = served(1, mine, a_end_moved, far)
        late = [move(one, first_pairs(wholes)), two, move(two, second_pairs(wholes))]
        parts = [early, early_other] + near + late
        cases = [([0], [1]), ([5], [6]), ([5], [7]), ([2], [3]), ([2], [4])]
    else:
        normed, kept = layer_norm(pair, pair_mask, in_gain[None], in_bias[None])
        quarters = [[(0, planes // 4 * at, at, None) for at in range(4)]]
        shapes = [(planes // 4,)] * 4
        weights = arranged(proj_weight)
        pieces = side(quarters, shapes, weights[1], [kept])
        lefts = side(quarters, shapes, weights[0], [kept])
        gate = output_gate(normed, gate_weight)
        places = [[[(0, plane), (1, plane)] for plane in range(planes // 4)]]
        sums = []
        for piece, left in zip(pieces, lefts):
            gathered = lax.all_gather(piece, "rows")
            zero = jnp.zeros_like(left)
            product = jnp.stack(
                [
                    triangle(places, [left, zero], [gathered[at], zero])
                    for at in range(mesh_rows)
                ]
            )
            gathered = lax.all_to_all(product, "cols", 0, 0, tiled=True)
            sums.append(jnp.sum(gathered.astype(jnp.float32), axis=0))
        total = jnp.concatenate(sums, axis=0)
        parts, cases = [total, jnp.zeros_like(total)], [([0], [1])]
    return finish(cases, parts, gain, shift, out_weight, gate)


def solution(mesh):
    tile = P(("groups", "rows"), "cols", None)
    return jax.shard_map(
        functools.partial(per_device, mesh.shape["rows"], mesh.shape["cols"]),
        mesh=mesh,
        in_specs=(tile, P(("groups", "rows"), "cols")) + (P(),) * 7,
        out_specs=tile,
        check_vma=False,
    )
```

```python
import functools

import jax
import jax.numpy as jnp
from jax import lax
from jax.experimental import pallas as pl
from jax.experimental.pallas import tpu as pltpu
from jax.sharding import PartitionSpec as P

EPS = 1e-05
VMEM = pl.BlockSpec(memory_space=pltpu.VMEM)
HBM = pl.BlockSpec(memory_space=pltpu.HBM)
STEP = 16


def place():
    row, col = lax.axis_index("rows"), lax.axis_index("cols")
    whole = col % 2 == row % 2
    early, middle = col // 2 == row // 2, (row == 1) | (row == 2)
    late = jnp.where(whole == middle, 4, jnp.where(middle, 2, 3))
    case = jnp.where(early, jnp.where(whole, 0, 1), late)
    return whole.astype(jnp.int32), ~early, case


def call(body, out_shape, in_specs, out_specs, scratch, limit=12):
    return pl.pallas_call(
        body,
        out_shape=out_shape,
        in_specs=in_specs,
        out_specs=out_specs,
        scratch_shapes=scratch,
        compiler_params=pltpu.CompilerParams(vmem_limit_bytes=limit * 1024 * 1024),
        cost_estimate=pl.CostEstimate(flops=1, bytes_accessed=1, transcendentals=0),
    )


def sigmoid(values):
    return 0.5 * jnp.tanh(0.5 * values) + 0.5


def dot(left, right, dims):
    return lax.dot_general(left, right, (dims, ((), ())), preferred_element_type=jnp.float32)


def split(values):
    high = values.astype(jnp.bfloat16)
    low = (values - high.astype(jnp.float32)).astype(jnp.bfloat16)
    return jnp.concatenate([high, low], axis=1)


def norm_body(pair_ref, mask_ref, gain_ref, shift_ref, out_ref, kept_ref, *scratch):
    held, made, kept, mask, gain_held, shift_held, sems = scratch
    rows, cols, channels = held.shape
    steps = sems.shape[1] - 3
    step = rows // steps
    spans = [pl.ds(at * step, step) for at in range(steps)]
    small = [
        pltpu.make_async_copy(mask_ref, mask, sems.at[0, steps]),
        pltpu.make_async_copy(gain_ref, gain_held, sems.at[0, steps + 1]),
        pltpu.make_async_copy(shift_ref, shift_held, sems.at[0, steps + 2]),
    ]
    loads = [
        pltpu.make_async_copy(pair_ref.at[span], held.at[span], sems.at[0, at])
        for at, span in enumerate(spans)
    ]
    for copy in loads[:1] + small + loads[1:]:
        copy.start()
    ones = jnp.full((2 * channels, channels), 1.0 / channels, jnp.bfloat16)
    for copy in small:
        copy.wait()
    gain, shift = gain_held[...], shift_held[...]
    stores = []
    for at, span in enumerate(spans):
        loads[at].wait()
        values = held[span].reshape(step * cols, channels)
        centered = values - dot(split(values), ones, ((1,), (0,)))
        squares = (centered * centered).astype(jnp.bfloat16)
        spread = dot(squares, ones[:channels], ((1,), (0,)))
        normed = centered * lax.rsqrt(spread + EPS) * gain + shift
        keep = mask[span].astype(jnp.float32).T
        for row in range(step):
            tile = normed[row * cols : (row + 1) * cols] * keep[:, row : row + 1]
            kept[at * step + row] = tile.astype(jnp.bfloat16)
        made[span] = normed.astype(jnp.bfloat16).reshape(step, cols, channels)
        stores += [
            pltpu.make_async_copy(kept.at[span], kept_ref.at[span], sems.at[1, at]),
            pltpu.make_async_copy(made.at[span], out_ref.at[span], sems.at[2, at]),
        ]
        stores[-2].start()
        stores[-1].start()
    for copy in stores:
        copy.wait()


def layer_norm(pair, mask, gain, shift, steps=2):
    half = pltpu.VMEM(pair.shape, jnp.bfloat16)
    return call(
        norm_body,
        [jax.ShapeDtypeStruct(pair.shape, jnp.bfloat16)] * 2,
        [HBM] * 4,
        [HBM] * 2,
        [
            pltpu.VMEM(pair.shape, jnp.float32),
            half,
            half,
            pltpu.VMEM(mask.shape, jnp.int32),
            pltpu.VMEM(gain.shape, jnp.float32),
            pltpu.VMEM(shift.shape, jnp.float32),
            pltpu.SemaphoreType.DMA((3, steps + 3)),
        ],
        limit=58,
    )(pair, mask, gain, shift)


def gate_body(normed_ref, weight_ref, out_ref, held, sems):
    rows, cols, channels = normed_ref.shape
    weight = weight_ref[...]
    copies = []
    for at in range(rows // STEP):
        span = pl.ds(at * STEP, STEP)
        values = dot(normed_ref[span].reshape(STEP * cols, channels), weight, ((1,), (0,)))
        held[span] = sigmoid(values).reshape(STEP, cols, channels)
        copies.append(pltpu.make_async_copy(held.at[span], out_ref.at[span], sems.at[at]))
        copies[-1].start()
    for copy in copies:
        copy.wait()


def output_gate(normed, weight):
    return call(
        gate_body,
        jax.ShapeDtypeStruct(normed.shape, jnp.float32),
        [VMEM, VMEM],
        HBM,
        [
            pltpu.VMEM(normed.shape, jnp.float32),
            pltpu.SemaphoreType.DMA((normed.shape[0] // STEP,)),
        ],
    )(normed, weight)


def side_body(cases, count, weight_ref, *refs):
    tiles, outs, held = refs[:count], refs[count:-1], refs[-1]
    rows, cols, channels = tiles[0].shape
    planes = channels // 2
    steps = rows // STEP
    spans = [pl.ds(at * STEP, STEP) for at in range(steps)]
    zero = jnp.zeros((cols, channels), jnp.bfloat16)

    def project(tile, writes):
        weight = weight_ref[...]
        for at, span in enumerate(spans):
            for row in range(0, STEP, 2):
                parts = []
                for more in range(2):
                    value = tiles[tile][at * STEP + row + more]
                    parts += [jnp.concatenate([value, zero], 1), jnp.concatenate([zero, value], 1)]
                both = dot(weight, jnp.concatenate(parts, axis=0), ((1,), (1,)))
                for more in range(2):
                    values = both[:, 2 * cols * more : 2 * cols * (more + 1)]
                    held[pl.ds(row + more, planes, stride=STEP), :] = (
                        sigmoid(values[planes:]) * values[:planes]
                    )
            for first, out, index in writes:
                out_ref = outs[out] if index is None else outs[out].at[index]
                number = out_ref.shape[0]
                value = held[first * STEP : (first + number) * STEP, :]
                value = value.reshape(number, STEP, 2 * cols)
                out_ref[:, span, :] = value.astype(jnp.bfloat16)

    def work(jobs):
        for tile, writes in jobs:
            project(tile, writes)

    if len(cases) == 1:
        work(cases[0])
    else:
        whole = place()[0]
        for value, jobs in enumerate(cases):
            if jobs:
                pl.when(whole == value)(functools.partial(work, jobs))


def side(cases, shapes, weight, tiles):
    rows, cols, channels = tiles[0].shape
    return call(
        functools.partial(side_body, cases, len(tiles)),
        [jax.ShapeDtypeStruct(shape + (rows, 2 * cols), jnp.bfloat16) for shape in shapes],
        [VMEM] * (1 + len(tiles)),
        [VMEM] * len(shapes),
        [pltpu.VMEM((channels // 2 * STEP, 2 * cols), jnp.float32)],
    )(weight, *tiles)


def paired(tiles):
    low = lax.broadcasted_iota(jnp.int32, tiles[0].shape, 1) < tiles[0].shape[1] // 2
    zero = jnp.zeros(tiles[0].shape, jnp.bfloat16)
    first = jnp.concatenate([jnp.where(low, tile, zero) for tile in tiles], axis=1)
    second = jnp.concatenate([jnp.where(low, zero, tile) for tile in tiles], axis=1)
    return jnp.concatenate([first, second], axis=0)


def triangle_body(cases, *refs):
    left, right, out_ref = refs[:2], refs[2:-1], refs[-1]

    def work(places):
        for plane, place in enumerate(places):
            first = jnp.concatenate([ref[plane] for ref in left], axis=1)
            second = paired([right[at[0]][at[1:]] for at in place])
            value = dot(first, second, ((1,), (1,)))
            out_ref[plane] = value.astype(jnp.bfloat16)

    if len(cases) == 1:
        work(cases[0])
    else:
        whole = place()[0]
        for case, places in enumerate(cases):
            if places:
                pl.when(whole == case)(functools.partial(work, places))


def triangle(cases, left, right):
    planes, rows, lanes = left[0].shape
    return call(
        functools.partial(triangle_body, cases),
        jax.ShapeDtypeStruct((planes, rows, 2 * rows), jnp.bfloat16),
        [VMEM] * (2 + len(right)),
        VMEM,
        [],
    )(*left, *right)


def served_body(start, order, *refs):
    mine, ends, right, outs = refs[:2], refs[2:4], refs[4:-2], refs[-2:]
    right = right if len(right) == 2 else [right[0].at[tile] for tile in order]
    rows = mine[0].shape[1]

    def work(firsts):
        for at in range(outs[0].shape[0]):
            both = [
                jnp.concatenate([ref[start + at] for ref in first], axis=1) for first in firsts
            ]
            second = paired([ref[at] for ref in right])
            value = dot(jnp.concatenate(both, axis=0), second, ((1,), (1,)))
            value = value.astype(jnp.bfloat16)
            outs[0][at] = value[:rows]
            outs[1][at] = value[rows:]

    whole, owner, _ = place()

    @pl.when((whole == 0) & owner)
    def _():
        work([ends, mine])

    @pl.when((whole == 0) & ~owner)
    def _():
        work([mine, ends])


def served(start, order, mine, ends, right):
    count, rows, _ = right[0].shape[-3:]
    return call(
        functools.partial(served_body, start, order),
        [jax.ShapeDtypeStruct((count, rows, 2 * rows), jnp.bfloat16)] * 2,
        [VMEM] * (4 + len(right)),
        [VMEM] * 2,
        [],
    )(*mine, *ends, *right)


def finish_body(cases, *refs):
    parts, (gain_ref, shift_ref, weight_ref, gate_ref, out_ref) = refs[:-10], refs[-10:-5]
    total, held, made, gate, sems = refs[-5:]
    planes, _, lanes = total.shape
    rows = gate.shape[0]
    steps = rows // STEP
    width = lanes // 2
    weight = weight_ref[...]
    spans = [pl.ds(at * STEP, STEP) for at in range(steps)]
    mine = place()[2] if len(cases) > 1 else 0
    loads = [
        pltpu.make_async_copy(gate_ref.at[span], gate.at[span], sems.at[at])
        for at, span in enumerate(spans)
    ]
    for load in loads:
        load.start()

    def mean(values):
        return (values + pltpu.roll(values, width, 1)) * (1.0 / (2 * planes))

    def add(first, second):
        ones = [(index, at) for index in first for at in range(parts[index].shape[0])]
        twos = [(index, at) for index in second for at in range(parts[index].shape[0])]
        for plane in range(planes):
            (one, here), (two, there) = ones[plane], twos[plane]
            value = parts[one][here].astype(jnp.float32)
            total[plane] = value + parts[two][there].astype(jnp.float32)

    for case, terms in enumerate(cases):
        pl.when(mine == case)(functools.partial(add, *terms))

    for at, span in enumerate(spans):
        added = jnp.zeros((STEP, lanes), jnp.float32)
        for plane in range(planes):
            added = added + total[plane, span]
        middle = mean(added)
        added = jnp.zeros((STEP, lanes), jnp.float32)
        for plane in range(planes):
            centered = total[plane, span] - middle
            added = added + centered * centered
        scale = lax.rsqrt(mean(added) + EPS)
        for plane in range(planes):
            normed = (total[plane, span] - middle) * scale * gain_ref[plane] + shift_ref[plane]
            held[pl.ds(plane, STEP, stride=planes), :] = normed
        loads[at].wait()
        for row in range(STEP):
            tile = held[row * planes : (row + 1) * planes, :].T.astype(jnp.bfloat16)
            update = dot(tile[:width], weight[:planes], ((1,), (0,)))
            update += dot(tile[width:], weight[planes:], ((1,), (0,)))
            made[at * STEP + row] = update * gate[at * STEP + row]
        pltpu.make_async_copy(made.at[span], out_ref.at[span], sems.at[steps + at]).start()
    for at, span in enumerate(spans):
        pltpu.make_async_copy(made.at[span], out_ref.at[span], sems.at[steps + at]).wait()


def finish(cases, parts, gain, shift, weight, gate):
    planes, _, lanes = gain.shape
    rows = gate.shape[0]
    return call(
        functools.partial(finish_body, cases),
        jax.ShapeDtypeStruct(gate.shape, jnp.float32),
        [VMEM] * (len(parts) + 3) + [HBM],
        HBM,
        [
            pltpu.VMEM((planes, rows, lanes), jnp.float32),
            pltpu.VMEM((planes * STEP, lanes), jnp.float32),
            pltpu.VMEM(gate.shape, jnp.float32),
            pltpu.VMEM(gate.shape, jnp.float32),
            pltpu.SemaphoreType.DMA((2 * rows // STEP,)),
        ],
    )(*parts, gain, shift, weight, gate)


def planes_of(vector, width):
    return jnp.repeat(vector.reshape(2, -1).T, width, axis=1)[:, None, :]


def arranged(weight):
    channels = weight.shape[0]
    weight = weight.reshape(channels, 2, 2, 2, channels // 2).transpose(1, 2, 4, 3, 0)
    return weight.reshape(2, channels, 2 * channels)


def per_device(
    mesh_rows,
    mesh_cols,
    pair,
    pair_mask,
    in_gain,
    in_bias,
    proj_weight,
    gate_weight,
    out_gain,
    out_bias,
    out_weight,
):
    rows, cols, channels = pair.shape
    planes = channels // 2
    gain, shift = planes_of(out_gain, cols), planes_of(out_bias, cols)

    if mesh_rows == 4 and mesh_cols == 4:
        both = ("rows", "cols")
        at = lambda z, x, h: z * 4 + 2 * x + h
        places = [(z, x, h) for z in range(4) for x in range(2) for h in range(2)]
        flip = [(at(z, x, h), at(z, x, 1 - h)) for z, x, h in places]
        wholes = [place for place in places if place[2] == place[0] % 2]
        others = [place for place in places if place[2] != place[0] % 2]
        middles = lambda some: [place for place in some if place[0] in (1, 2)]
        partners = [(at(z, x, h), at(z ^ 1, x, h)) for z, x, h in wholes]
        across = [(at(z, x, h), at(3 - z, x, 1 - h)) for z, x, h in middles(others)]
        two_hops = [(at(z, x, h), at(2 - z // 3, x, 1 - h)) for z, x, h in wholes if z in (0, 3)]
        owner = lambda z: 1 - z // 2
        early_pairs = lambda some: [
            (at(z, x, h), at(z, 1 - x, h)) for z, x, h in some if x == owner(z)
        ]
        first_pairs = lambda flipped: [
            (at(z, x, h), at(z ^ 1, x, h ^ flipped) if x == owner(z) else at(z, 1 - x, h ^ flipped))
            for z, x, h in middles(others)
        ]
        second_pairs = lambda flipped: [
            (at(z, x, h), at(z ^ 1, 1 - x, h ^ flipped))
            for z, x, h in middles(others)
            if x != owner(z)
        ]
        beside = [(at(z, x, h), at(z, x, 1 - h)) for z, x, h in middles(others) if x == owner(z)]
        move = lambda array, pairs: lax.ppermute(array, both, pairs)
        tie = lax.optimization_barrier
        cut = 3 * planes // 4
        full = [(0, [(0, 0, None)])]
        cut_tiles = [(tile, [(0, 0, tile), (cut, 1, tile)]) for tile in (0, 1)]
        plain = [[(0, plane), (1, plane)] for plane in range(planes)]
        cut_plain = [
            [(plane // cut, tile, plane % cut) for tile in (0, 1)] for plane in range(planes)
        ]
        one_side = lambda column, cases, tile: side(cases, [(planes,)], weights[column], [tile])[0]

        normed, kept = layer_norm(pair, pair_mask, in_gain[None], in_bias[None])
        kept_other = move(kept, flip)
        partner = move(kept, partners)
        near_other = move(kept, across)
        partner_other = move(kept_other, partners)
        near = move(kept_other, across)
        kept, proj_weight = tie((kept, proj_weight))
        weights = arranged(proj_weight)
        b_own = side(
            [[], cut_tiles], [(2, cut), (2, planes - cut)], weights[1], [kept, kept_other]
        )
        kept, b_own = tie((kept, b_own))
        a_own = one_side(0, [full], kept)
        a_other = one_side(0, [full], kept_other)
        mine = [a_own, a_other]
        own = triangle([[], cut_plain], mine, b_own)
        gate = output_gate(normed, gate_weight)
        partner, mine, own, gate, gain, shift = tie((partner, mine, own, gate, gain, shift))
        near_other, partner = tie((near_other, partner))
        a_end = one_side(0, [full, []], partner)
        b_near_other = one_side(1, [full, []], near_other)
        partner_other, a_end, b_near_other = tie((partner_other, a_end, b_near_other))
        near, partner_other, own, b_own = tie((near, partner_other, own, b_own))
        far = [move(part, two_hops) for part in b_own]
        own_other = move(own, early_pairs(wholes))
        a_end_other = one_side(0, [full, []], partner_other)
        b_near = one_side(1, [full, []], near)
        ends = [a_end, a_end_other]
        one, two = served(0, None, mine, ends, [b_near, b_near_other])
        near = [move(one, first_pairs(0)), two, move(two, second_pairs(0))]
        partner, partner_other, one, own_other = tie((partner, partner_other, one, own_other))
        b_partner = one_side(1, [full, []], partner)
        b_partner_other = one_side(1, [full, []], partner_other)
        partner = triangle([plain, []], mine, [b_partner, b_partner_other])
        partner_sent = move(partner, early_pairs(others))
        ends, partner = tie((ends, partner))
        one, two = served(0, (1, 0), mine, ends, far[:1])
        late = [move(one, first_pairs(1)), move(two, second_pairs(1) + beside)]
        ends, one, near = tie((ends, one, near))
        one, two = served(cut, (1, 0), mine, ends, far[1:])
        last = [move(one, first_pairs(1)), move(two, second_pairs(1) + beside)]
        late, partner_sent, gain, shift = tie((late, partner_sent, gain, shift))
        parts = [own, own_other, partner, partner_sent] + near + late + last
        cases = [([0], [1]), ([2], [3]), ([4], [5]), ([4], [6]), ([7, 9], [8, 10])]
    else:
        normed, kept = layer_norm(pair, pair_mask, in_gain[None], in_bias[None])
        quarters = [[(0, [(planes // 4 * at, at, None) for at in range(4)])]]
        shapes = [(planes // 4,)] * 4
        weights = arranged(proj_weight)
        pieces = side(quarters, shapes, weights[1], [kept])
        lefts = side(quarters, shapes, weights[0], [kept])
        gate = output_gate(normed, gate_weight)
        places = [[[(0, plane), (1, plane)] for plane in range(planes // 4)]]
        sums = []
        for piece, left in zip(pieces, lefts):
            gathered = lax.all_gather(piece, "rows")
            zero = jnp.zeros_like(left)
            product = jnp.stack(
                [
                    triangle(places, [left, zero], [gathered[at], zero])
                    for at in range(mesh_rows)
                ]
            )
            gathered = lax.all_to_all(product, "cols", 0, 0, tiled=True)
            sums.append(jnp.sum(gathered.astype(jnp.float32), axis=0))
        total = jnp.concatenate(sums, axis=0)
        parts, cases = [total, jnp.zeros_like(total)], [([0], [1])]
    return finish(cases, parts, gain, shift, out_weight, gate)


def solution(mesh):
    tile = P(("groups", "rows"), "cols", None)
    return jax.shard_map(
        functools.partial(per_device, mesh.shape["rows"], mesh.shape["cols"]),
        mesh=mesh,
        in_specs=(tile, P(("groups", "rows"), "cols")) + (P(),) * 7,
        out_specs=tile,
        check_vma=False,
    )
```
